256 devices in a mesh: src: 8 (over x, core), rcv: 32 (over z, y).
Axes of the slice: x: 4, y: 4, z: 8, core: 2. Of those that a mesh axis runs over, the one named last changes fastest.
Arguments:
- data: bfloat16 [3, 2, 4096, 4096], P(None, None, 'src', 'rcv'), may hold values from -0.75 to 0.75
Outputs:
- predicted: bfloat16 [3, 2, 4096, 4096], P(None, None, 'src', 'rcv')
The draws below stay inside these ranges and needn't reach their ends.
All inputs are finite; a program needn't handle non-finite values.
Results may differ from the reference program's by a relative error of at most 0.001.
Values may be sent and summed in bfloat16 or wider, within the bound.
A program may use at most 128 MiB of HBM per device.

```python
import jax
import jax.numpy as jnp
from jax import lax

S = 4096
FREQS = 3


def shard_levels(stream_key, shape, shards, low, high):
    gain = 1.0
    for axis_at, blocks in shards:
        heights = jax.random.uniform(jax.random.fold_in(jax.random.fold_in(stream_key, 6), axis_at), (blocks,), jnp.float32, low / len(shards), high / len(shards))
        gain = gain * jnp.repeat(jnp.exp(heights), shape[axis_at] // blocks).reshape((-1,) + (1,) * (len(shape) - 1 - axis_at))
    return gain


def scatter_about(own_key, extent, scale, bound, cuts=(), dtype=jnp.bfloat16):
    result = scale * jax.random.normal(own_key, extent, jnp.float32)
    if cuts:
        result = result * shard_levels(own_key, extent, cuts, -0.22, 0.18)
    return jnp.clip(result, -bound, bound).astype(dtype)


def setup_inputs(seed: int = 0) -> dict:
    keys = jax.random.split(jax.random.key(seed), 2)
    data = scatter_about(keys[0], (FREQS, 2, S, S), 0.125, 0.75, ((2, 8), (3, 32)))
    return dict(data=data)


def complex_square(panel):
    real_in = panel[0].astype(jnp.float32)
    imag_in = panel[1].astype(jnp.float32)
    high = lax.Precision.HIGHEST
    real_part = jnp.dot(real_in, real_in, precision=high, preferred_element_type=jnp.float32) - jnp.dot(imag_in, imag_in, precision=high, preferred_element_type=jnp.float32)
    imag_part = jnp.dot(real_in, imag_in, precision=high, preferred_element_type=jnp.float32) + jnp.dot(imag_in, real_in, precision=high, preferred_element_type=jnp.float32)
    return jnp.stack([real_part, imag_part]).astype(jnp.bfloat16)


def reference(data):
    return lax.map(complex_square, data)
```

```python
import functools

import jax
import jax.numpy as jnp
from jax import lax
from jax.experimental import pallas as pl
from jax.experimental.pallas import tpu as pltpu
from jax.sharding import PartitionSpec as P

MESH = pl.DeviceIdType.MESH
NX, NY, NZ = 4, 4, 8
ROWS, COLS = 512, 128
HALF = ROWS // 2
PARTS = 2
PIECE = ROWS // PARTS
ORDER = ((0, 0), (1, 1), (0, 1), (1, 0))


def hops(direction, unit):
    return 4 if direction == unit else 3


def kernel(d, o, left_a, right_a, left_b, right_b, acc_a, acc_b, part, out_a, out_b,
           own_left_s, own_left_r, own_right_s, own_right_r, own_a_s, own_a_r, local_sem,
           zb_s, zb_r, za_s, za_r, cb_s, cb_r, ca_s, ca_r, xb_s, xb_r, xa_s, xa_r,
           part_s, part_r, fin_a_s, fin_a_r, fin_b_s, fin_b_r):
    src, rcv = lax.axis_index("src"), lax.axis_index("rcv")
    x, c = src // 2, src % 2
    z, y = rcv // NY, rcv % NY
    h, low = y // 2, y % 2

    def dev(x, c, z, y):
        return (x * 2 + c, z * NY + y)

    z_next = (dev(x, c, (z + 1) % NZ, y), dev(x, c, (z + NZ - 1) % NZ, y))
    x_next = (dev((x + 1) % NX, c, z, y), dev((x + NX - 1) % NX, c, z, y))
    partner = dev(x, 1 - c, z, y)

    barrier = pltpu.get_barrier_semaphore()
    friends = list(z_next) + list(x_next) + [partner]
    for step in range(1, NY):
        for core in range(2):
            friends.append(dev(x, (c + core) % 2, z, (y + step) % NY))
    for friend in friends:
        pl.semaphore_signal(barrier, inc=1, device_id=friend, device_id_type=MESH)
    pl.semaphore_wait(barrier, len(friends))

    sent = []

    def send(src_ref, dst_ref, s_sem, r_sem, device, here=None):
        copy = pltpu.make_async_remote_copy(
            src_ref=src_ref, dst_ref=dst_ref, send_sem=s_sem, recv_sem=r_sem, device_id=device, device_id_type=MESH)
        if here is None:
            copy.start()
        else:
            pl.when(jnp.logical_not(here))(copy.start)
            pl.when(here)(pltpu.make_async_copy(src_ref, dst_ref, r_sem).start)
        sent.append((copy, here))

    def got(dst_ref, r_sem):
        pltpu.make_async_copy(dst_ref, dst_ref, r_sem).wait()

    def piece(q):
        return pl.ds(q * PIECE, PIECE)

    for u in range(2):
        send(d.at[1, u], left_b.at[z, low, u], own_left_s.at[u], own_left_r.at[u], dev(x, low, z, h * 2 + c), low == c)
    for half in range(2):
        for k in range(2):
            send(d.at[1, :, pl.ds(half * HALF, HALF)], right_b.at[x, c, low], own_right_s.at[half, k], own_right_r.at[c, low],
                 dev(x, h, z, half * 2 + k), jnp.logical_and(h == c, y == half * 2 + k))

    def block_b(zz, u, q):
        return left_b.at[zz, c, u, piece(q)]

    def block_a(zz, u, q):
        return left_a.at[zz, 2 * c + u, :, piece(q)]

    def own_a(u, q):
        return right_a.at[x, low, u, :, piece(q)]

    def z_first(block, source, s_sem, r_sem, c_s, c_r):
        for q in range(PARTS):
            for direction, u in ORDER:
                send(source(u, q), block(z, u, q), s_sem.at[direction, 0, u, q], r_sem.at[direction, 0, u, q], z_next[direction])
            for u in range(2):
                send(source(u, q), block(z, u, q), c_s.at[0, u, q], c_r.at[0, u, q], partner)

    def come(direction, step):
        return (z + NZ - step) % NZ if direction == 0 else (z + step) % NZ

    def away(direction, step):
        return (NZ - step) % NZ if direction == 0 else step

    def z_arrive(block, s_sem, r_sem, c_s, c_r, step, parts=range(PARTS)):
        for q in parts:
            for direction, u in ORDER:
                if step > hops(direction, u):
                    continue
                here = block(come(direction, step), u, q)
                got(here, r_sem.at[direction, step - 1, u, q])
                if step < hops(direction, u):
                    send(here, here, s_sem.at[direction, step, u, q], r_sem.at[direction, step, u, q], z_next[direction])
                k = away(direction, step)
                send(here, here, c_s.at[k, u, q], c_r.at[k, u, q], partner)

    def c_arrive(wide, c_r, k, parts=range(PARTS)):
        for q in parts:
            for u in range(2):
                got(wide((z + k) % NZ, u, q), c_r.at[k, u, q])

    def other_b(zz, u, q):
        return left_b.at[zz, 1 - c, u, piece(q)]

    def other_a(zz, u, q):
        return left_a.at[zz, 2 * (1 - c) + u, :, piece(q)]

    zb = (zb_s, zb_r, cb_s, cb_r)
    za = (za_s, za_r, ca_s, ca_r)

    def x_first(right, s_sem, r_sem):
        for k in range(2):
            for p in range(2):
                for direction in range(2):
                    send(right.at[x, k, p], right.at[x, k, p], s_sem.at[direction, 0, k, p], r_sem.at[direction, 0, k, p], x_next[direction])

    def x_second(right, s_sem, r_sem):
        for k in range(2):
            for p in range(2):
                for direction in range(2):
                    xx = (x + NX - 1) % NX if direction == 0 else (x + 1) % NX
                    here = right.at[xx, k, p]
                    got(here, r_sem.at[direction, 0, k, p])
                    if p == direction:
                        send(here, here, s_sem.at[direction, 1, k, p], r_sem.at[direction, 1, k, p], x_next[direction])

    def x_last(right, r_sem):
        for k in range(2):
            for direction in range(2):
                got(right.at[(x + 2) % NX, k, direction], r_sem.at[direction, 1, k, direction])

    def multiply(left, width, right, acc, zz, q, rows):
        xx, k = zz // 2, zz % 2
        at = pl.ds(q * rows, rows)
        lr = jnp.concatenate([left[zz, j, 0, at, :] for j in range(width)], axis=1)
        li = jnp.concatenate([left[zz, j, 1, at, :] for j in range(width)], axis=1)
        rr = jnp.concatenate([right[xx, k, p, 0] for p in range(2)], axis=1)
        ri = jnp.concatenate([right[xx, k, p, 1] for p in range(2)], axis=1)

        def dot(a, b):
            return jnp.dot(a, b, preferred_element_type=jnp.float32)

        acc[0, at, :] += dot(lr, rr) - dot(li, ri)
        acc[1, at, :] += dot(lr, ri) + dot(li, rr)

    for u in range(2):
        got(left_b.at[z, c, u], own_left_r.at[u])
    z_first(block_b, lambda u, q: block_b(z, u, q), *zb)
    for k in range(2):
        for p in range(2):
            got(right_b.at[x, k, p], own_right_r.at[k, p])
    x_first(right_b, xb_s, xb_r)
    for half in range(2):
        for k in range(2):
            send(d.at[2 * half], right_a.at[x, c, low], own_a_s.at[half, k], own_a_r.at[c, low],
                 dev(x, h, z, half * 2 + k), jnp.logical_and(h == c, y == half * 2 + k))
    acc_a[...] = jnp.zeros_like(acc_a)
    acc_b[...] = jnp.zeros_like(acc_b)
    z_arrive(block_b, *zb, 1)
    x_second(right_b, xb_s, xb_r)
    z_arrive(block_b, *zb, 2)
    for k in range(2):
        for p in range(2):
            got(right_a.at[x, k, p], own_a_r.at[k, p])
    z_first(block_a, own_a, *za)
    x_first(right_a, xa_s, xa_r)
    keep = pltpu.make_async_copy(right_a.at[x, low], left_a.at[z, pl.ds(2 * c, 2)], local_sem)
    keep.start()
    z_arrive(block_b, *zb, 3)
    z_arrive(block_b, *zb, 4)
    x_last(right_b, xb_r)
    for k in range(NZ):
        c_arrive(other_b, cb_r, k)

    def whole_b(k, _):
        for q in range(2):
            multiply(left_b, 2, right_b, acc_b, (z + k) % NZ, q, HALF)
        return 0

    lax.fori_loop(0, NZ, whole_b, 0)
    send(acc_b.at[:, pl.ds((1 - h) * HALF, HALF)], part, part_s, part_r, dev(x, c, z, (y + 2) % NY))
    z_arrive(block_a, *za, 1)
    x_second(right_a, xa_s, xa_r)
    got(part, part_r)
    for p in range(2):
        for i in range(2):
            at = pl.ds(p * COLS, COLS)
            out_b[p, i] = (acc_b[i, pl.ds(pl.multiple_of(h * HALF, HALF), HALF), at] + part[i, :, at]).astype(jnp.bfloat16)
        send(out_b.at[p], o.at[1, :, pl.ds(h * HALF, HALF)], fin_b_s.at[p], fin_b_r.at[h],
             dev(x, low, z, 2 * c + p), jnp.logical_and(low == c, y == 2 * c + p))
    z_arrive(block_a, *za, 2)
    z_arrive(block_a, *za, 3)
    keep.wait()
    x_last(right_a, xa_r)
    for k in range(NZ):
        if k != 4:
            c_arrive(other_a, ca_r, k)

    def whole_a(k, _):
        for q in range(2):
            multiply(left_a, 4, right_a, acc_a, (z + k + 5) % NZ, q, HALF)
        return 0

    lax.fori_loop(0, NZ - 1, whole_a, 0)
    for q in range(PARTS):
        z_arrive(block_a, *za, 4, (q,))
        c_arrive(other_a, ca_r, 4, (q,))
        multiply(left_a, 4, right_a, acc_a, (z + 4) % NZ, q, PIECE)
        for p in range(2):
            for i in range(2):
                out_a[p, i, piece(q)] = acc_a[i, piece(q), pl.ds(p * COLS, COLS)].astype(jnp.bfloat16)
            send(out_a.at[p, :, piece(q)], o.at[2 * h, :, piece(q)], fin_a_s.at[p, q], fin_a_r.at[h, q],
                 dev(x, low, z, 2 * c + p), jnp.logical_and(low == c, y == 2 * c + p))
    for half in range(2):
        got(o.at[1, :, pl.ds(half * HALF, HALF)], fin_b_r.at[half])
        for q in range(PARTS):
            got(o.at[2 * half, :, piece(q)], fin_a_r.at[half, q])
    for copy, here in sent:
        if here is None:
            copy.wait_send()
        else:
            pl.when(jnp.logical_not(here))(copy.wait_send)


def local(data):
    bf16, f32 = jnp.bfloat16, jnp.float32
    sem = pltpu.SemaphoreType.DMA
    return pl.pallas_call(
        kernel,
        out_shape=jax.ShapeDtypeStruct(data.shape, data.dtype),
        in_specs=[pl.BlockSpec(memory_space=pltpu.VMEM)],
        out_specs=pl.BlockSpec(memory_space=pltpu.VMEM),
        scratch_shapes=[
            pltpu.VMEM((NZ, 4, 2, ROWS, COLS), bf16),
            pltpu.VMEM((NX, 2, 2, 2, ROWS, COLS), bf16),
            pltpu.VMEM((NZ, 2, 2, ROWS, COLS), bf16),
            pltpu.VMEM((NX, 2, 2, 2, HALF, COLS), bf16),
            pltpu.VMEM((2, ROWS, 2 * COLS), f32),
            pltpu.VMEM((2, ROWS, 2 * COLS), f32),
            pltpu.VMEM((2, HALF, 2 * COLS), f32),
            pltpu.VMEM((2, 2, ROWS, COLS), bf16),
            pltpu.VMEM((2, 2, HALF, COLS), bf16),
            sem((2,)), sem((2,)),
            sem((2, 2)), sem((2, 2)),
            sem((2, 2)), sem((2, 2)),
            sem,
            sem((2, 4, 2, PARTS)), sem((2, 4, 2, PARTS)),
            sem((2, 4, 2, PARTS)), sem((2, 4, 2, PARTS)),
            sem((NZ, 2, PARTS)), sem((NZ, 2, PARTS)),
            sem((NZ, 2, PARTS)), sem((NZ, 2, PARTS)),
            sem((2, 2, 2, 2)), sem((2, 2, 2, 2)),
            sem((2, 2, 2, 2)), sem((2, 2, 2, 2)),
            sem, sem,
            sem((2, PARTS)), sem((2, PARTS)),
            sem((2,)), sem((2,)),
        ],
        compiler_params=pltpu.CompilerParams(collective_id=0, has_side_effects=True, vmem_limit_bytes=48 << 20),
        cost_estimate=pl.CostEstimate(flops=6442450944, bytes_accessed=1572864, transcendentals=0),
    )(data)


def solution(mesh):
    spec = P(None, None, "src", "rcv")
    return jax.shard_map(local, mesh=mesh, in_specs=(spec,), out_specs=spec, check_vma=False)
```

```python
import functools

import jax
import jax.numpy as jnp
from jax import lax
from jax.experimental import pallas as pl
from jax.experimental.pallas import tpu as pltpu
from jax.sharding import PartitionSpec as P

MESH = pl.DeviceIdType.MESH
NX, NY, NZ = 4, 4, 8
ROWS, COLS = 512, 128
HALF = ROWS // 2
PARTS = 2
PIECE = ROWS // PARTS


def hops(direction, n):
    return 4 if direction == n else 3


def kernel(d, o, left_a, right_a, left_b, right_b, acc_a, acc_b, part, out_a, out_b,
           own_left_s, own_left_r, own_b_s, own_b_r, own_a_s, own_a_r, give_s, give_r, keep_sem,
           zb_s, zb_r, za_s, za_r, cb_s, cb_r, ca_s, ca_r, xb_s, xb_r, xa_s, xa_r, tb_s, tb_r, ta_s, ta_r,
           part_s, part_r, fin_a_s, fin_a_r, fin_b_s, fin_b_r):
    src, rcv = lax.axis_index("src"), lax.axis_index("rcv")
    x, c = src // 2, src % 2
    z, y = rcv // NY, rcv % NY
    h = y // 2
    low = (y + h) % 2
    pair, across = 2 * h + (y + 1) % 2, NY - 1 - y

    def dev(x, c, z, y):
        return (x * 2 + c, z * NY + y)

    z_next = (dev(x, c, (z + 1) % NZ, y), dev(x, c, (z + NZ - 1) % NZ, y))
    x_next = (dev((x + 1) % NX, c, z, y), dev((x + NX - 1) % NX, c, z, y))
    partner = dev(x, 1 - c, z, y)

    barrier = pltpu.get_barrier_semaphore()
    friends = list(z_next) + list(x_next) + [partner]
    for step in range(1, NY):
        for core in range(2):
            friends.append(dev(x, (c + core) % 2, z, (y + step) % NY))
    for friend in friends:
        pl.semaphore_signal(barrier, inc=1, device_id=friend, device_id_type=MESH)
    acc_a[...] = jnp.zeros_like(acc_a)
    acc_b[...] = jnp.zeros_like(acc_b)
    pl.semaphore_wait(barrier, len(friends))

    def piece(q):
        return pl.ds(q * PIECE, PIECE)

    def got(dst_ref, r_sem):
        pltpu.make_async_copy(dst_ref, dst_ref, r_sem).wait()

    def send(sent, src_ref, dst_ref, s_sem, r_sem, device, here=None):
        copy = pltpu.make_async_remote_copy(
            src_ref=src_ref, dst_ref=dst_ref, send_sem=s_sem, recv_sem=r_sem, device_id=device, device_id_type=MESH)
        if here is None:
            copy.start()
        else:
            pl.when(jnp.logical_not(here))(copy.start)
            pl.when(here)(pltpu.make_async_copy(src_ref, dst_ref, r_sem).start)
        sent.append((copy, here))

    def all_sent(sent):
        for copy, here in sent:
            if here is None:
                copy.wait_send()
            else:
                pl.when(jnp.logical_not(here))(copy.wait_send)

    first = []
    stays = low == c
    send(first, d.at[1, :, pl.ds((1 - h) * HALF, HALF)], right_b.at[x, c, y], own_b_s.at[0, 1, 0], own_b_r.at[0, c, 1], dev(x, 1, z, across))
    for q in range(PARTS):
        send(first, d.at[1, :, piece(q)], left_b.at[z, y % 2, :, piece(q)], own_left_s.at[q], own_left_r.at[jnp.where(stays, 0, 1), q],
             dev(x, 0, z, jnp.where(stays, y, pair)), jnp.logical_and(stays, c == 0))
    send(first, d.at[1, :, pl.ds(h * HALF, HALF)], right_b.at[x, c, y], own_b_s.at[0, 0, 0], own_b_r.at[0, c, 0], dev(x, 1, z, y), c == 1)
    send(first, d.at[2 * (1 - h)], right_a.at[x, c, y], own_a_s.at[0, 1, 0], own_a_r.at[0, c, 1], dev(x, 1, z, across))
    send(first, d.at[2 * h], right_a.at[x, c, y], own_a_s.at[0, 0, 0], own_a_r.at[0, c, 0], dev(x, 1, z, y), c == 1)

    def column(n, m):
        base = y if n == 0 else pair
        return base if m == 0 else NY - 1 - base

    def low_column(n):
        near = jnp.where(h == 0, y, across)
        return near if n == 0 else 1 - near

    def block_b(zz, n, m, q):
        return left_b.at[zz, (y + n) % 2, :, piece(q)]

    def block_a(zz, n, m, q):
        return left_a.at[zz, column(n, m), :, piece(q)]

    zb = (block_b, 1, zb_s, zb_r, cb_s, cb_r)
    za = (block_a, 2, za_s, za_r, ca_s, ca_r)
    xb = (right_b, xb_s, xb_r, tb_s, tb_r)
    xa = (right_a, xa_s, xa_r, ta_s, ta_r)

    def run(core):
        sent = []
        give = functools.partial(send, sent)
        plan = []

        def at_time(time, action, *args):
            plan.append((time, functools.partial(action, *args)))

        def z_first(block, ms, s_sem, r_sem, c_s, c_r, n, m, q, back):
            here = block(z, n, m, q)
            for direction in range(2):
                give(here, here, s_sem.at[direction, 0, n, m, q], r_sem.at[direction, 0, n, m, q], z_next[direction])
            if back:
                give(here, here, c_s.at[0, n, m, q], c_r.at[0, n, m, q], partner)

        def z_arrive(block, ms, s_sem, r_sem, c_s, c_r, step, i, m, q):
            for direction in range(2):
                n = direction if i == 0 else 1 - direction
                zz = (z + NZ - step) % NZ if direction == 0 else (z + step) % NZ
                k = NZ - step if direction == 0 else step
                here = block(zz, n, m, q)
                got(here, r_sem.at[direction, step - 1, n, m, q])
                if step < hops(direction, n):
                    give(here, here, s_sem.at[direction, step, n, m, q], r_sem.at[direction, step, n, m, q], z_next[direction])
                give(here, here, c_s.at[k, n, m, q], c_r.at[k, n, m, q], partner)

        def start_b(n):
            for q in range(PARTS):
                got(block_b(z, n, 0, q), own_left_r.at[n, q])
                z_first(*zb, n, 0, q, True)

        def take_a(n, m):
            got(left_a.at[z, column(n, m)], give_r.at[n, m])

        def start_a(n, q):
            for m in range(2):
                z_first(*za, n, m, q, False)

        def left_ready(z_of, k, q):
            block, ms, _, _, _, c_r = z_of
            if core == 1 and (k or ms == 1):
                for n in range(2):
                    for m in range(ms):
                        got(block((z + k) % NZ, n, m, q), c_r.at[k, n, m, q])

        def own_second(right, s_sem, r_sem, k, m):
            here = right.at[x, k, column(0, m)]
            got(here, r_sem.at[0, k, m])
            give(here, here, s_sem.at[1, k, m], r_sem.at[1, k, m], dev(x, c, z, pair))

        def own_last(right, r_sem, k, m):
            got(right.at[x, k, column(1, m)], r_sem.at[1, k, m])

        def pass_on(right, t_s, t_r, slot, xx, k, n):
            here = right.at[xx, k, low_column(n)]
            give(here, here, t_s.at[slot, k, n], t_r.at[slot, k, n], partner)

        def x_first(right, s_sem, r_sem, t_s, t_r, n, m):
            for k in range(2):
                here = right.at[x, k, column(n, m)]
                for direction in range(2):
                    give(here, here, s_sem.at[direction, 0, k, n, m], r_sem.at[direction, 0, k, n, m], x_next[direction])
                if m == 1:
                    pass_on(right, t_s, t_r, 0, x, k, n)

        def x_arrive(right, s_sem, r_sem, t_s, t_r, k, n, m):
            for direction in range(2):
                xx = (x + NX - 1) % NX if direction == 0 else (x + 1) % NX
                here = right.at[xx, k, column(n, m)]
                got(here, r_sem.at[direction, 0, k, n, m])
                if n == direction:
                    give(here, here, s_sem.at[direction, 1, k, n, m], r_sem.at[direction, 1, k, n, m], x_next[direction])
                if m == 1:
                    pass_on(right, t_s, t_r, 1 + direction, xx, k, n)

        def x_last(right, s_sem, r_sem, t_s, t_r, k, m):
            xx = (x + 2) % NX
            for n in range(2):
                got(right.at[xx, k, column(n, m)], r_sem.at[n, 1, k, n, m])
                if m == 1:
                    pass_on(right, t_s, t_r, 3, xx, k, n)

        def give_left(n, m):
            here, there = right_a.at[x, low, column(n, m)], left_a.at[z, column(n, m)]
            give(here, there, give_s.at[n, m], give_r.at[n, m], partner)
            pltpu.make_async_copy(here, there, keep_sem.at[n, m]).start()

        def keep_left():
            for n in range(2):
                for m in range(2):
                    got(left_a.at[z, column(n, m)], keep_sem.at[n, m])

        def right_ready(x_of, slots):
            if core == 0:
                right, _, _, _, t_r = x_of
                for slot in slots:
                    for k in range(2):
                        for n in range(2):
                            got(right.at[(x + (0, 3, 1, 2)[slot]) % NX, k, low_column(n)], t_r.at[slot, k, n])

        def multiply(left, width, right, acc, zz, start, rows):
            xx, k = zz // 2, zz % 2
            at = pl.ds(start, rows)
            lr = jnp.concatenate([left[zz, j, 0, at, :] for j in range(width)], axis=1)
            li = jnp.concatenate([left[zz, j, 1, at, :] for j in range(width)], axis=1)
            rr = jnp.concatenate([right[xx, k, 2 * core + p, 0] for p in range(2)], axis=1)
            ri = jnp.concatenate([right[xx, k, 2 * core + p, 1] for p in range(2)], axis=1)

            def dot(a, b):
                return jnp.dot(a, b, preferred_element_type=jnp.float32)

            acc[0, at, :] += dot(lr, rr) - dot(li, ri)
            acc[1, at, :] += dot(lr, ri) + dot(li, rr)

        def whole_b():
            for k in range(NZ):
                for q in range(PARTS):
                    left_ready(zb, k, q)
            right_ready(xb, range(4))

            def one(k, _):
                for q in range(2):
                    multiply(left_b, 2, right_b, acc_b, (z + k) % NZ, q * HALF, HALF)
                return 0

            lax.fori_loop(0, NZ, one, 0)
            give(acc_b.at[:, pl.ds((1 - h) * HALF, HALF)], part, part_s, part_r, dev(x, c, z, across))

        def finish_b():
            got(part, part_r)
            for p in range(2):
                for i in range(2):
                    at = pl.ds(p * COLS, COLS)
                    out_b[p, i] = (acc_b[i, pl.ds(pl.multiple_of(h * HALF, HALF), HALF), at] + part[i, :, at]).astype(jnp.bfloat16)
                give(out_b.at[p], o.at[1, :, pl.ds(h * HALF, HALF)], fin_b_s.at[p], fin_b_r.at[h],
                     dev(x, low, z, 2 * c + p), jnp.logical_and(low == c, y == 2 * c + p))

        def chunks_a(start, stop, q, want=None):
            for k in range(start, stop + 1):
                left_ready(za, k % NZ, q)

            def one(k, _):
                zz = (z + k + start % NZ) % NZ
                if want is None:
                    multiply(left_a, 4, right_a, acc_a, zz, q * PIECE, PIECE)
                else:
                    far = (zz // 2 + NX - x) % NX == 2
                    pl.when(far if want else jnp.logical_not(far))(lambda: multiply(left_a, 4, right_a, acc_a, zz, q * PIECE, PIECE))
                return 0

            lax.fori_loop(0, stop + 1 - start, one, 0)

        def far_a(q):
            def one(k, _):
                multiply(left_a, 4, right_a, acc_a, ((x + 2) % NX) * 2 + k, q * PIECE, PIECE)
                return 0

            lax.fori_loop(0, 2, one, 0)

        def finish_a(q):
            for p in range(2):
                for i in range(2):
                    out_a[p, i, piece(q)] = acc_a[i, piece(q), pl.ds(p * COLS, COLS)].astype(jnp.bfloat16)
                give(out_a.at[p, :, piece(q)], o.at[2 * h, :, piece(q)], fin_a_s.at[p, q], fin_a_r.at[h, q],
                     dev(x, low, z, 2 * c + p), jnp.logical_and(low == c, y == 2 * c + p))

        hop = 1.9
        sub = 39.4 / PARTS
        begin_b = 1.7
        begin_a = begin_b + 19.7

        def z_time_b(step, i, q):
            return begin_b + 5.6 * (step - 1) + 2.8 * (i + (q + 1) / PARTS) + hop

        def z_time_a(step, i, m, q):
            if q < PARTS - 2:
                return begin_a + sub * (q + (step - 1 + (2 * i + m + 1) / 4) / 3.5) + hop
            ahead = sub / 3.5
            if q == PARTS - 2:
                return begin_a + sub * (q + (step - 1 + (2 * i + m + 1) / 4) / 3.5) + hop + (ahead if step > 1 else 0)
            if step == 1:
                return begin_a + sub * q + ahead * (1 + (2 * i + m) / 4) - 2.5
            return begin_a + sub * q + ahead * (step - 1 + (2 * i + m + 1) / 4) + hop

        if core == 0:
            at_time(1, start_b, 0)
            at_time(4.5, start_b, 1)
            for m in range(2):
                at_time(17.4 + m / 100, take_a, 0, m)
                at_time(21.5 + m / 100, take_a, 1, m)
            for q in range(PARTS):
                first_time = 0 if q == 0 else begin_a + sub * (q - 1) + 2.5
                at_time(max(17.5, first_time), start_a, 0, q)
                at_time(max(21.6, first_time + 0.01), start_a, 1, q)
            for step in range(1, 5):
                for i in range(2 if step < 4 else 1):
                    for q in range(PARTS):
                        at_time(z_time_b(step, i, q), z_arrive, *zb, step, i, 0, q)
                        for m in range(2):
                            at_time(z_time_a(step, i, m, q), z_arrive, *za, step, i, m, q)
        else:
            for k in range(2):
                at_time(1.5, own_second, right_b, own_b_s, own_b_r, k, 0)
                at_time(4.6, own_second, right_b, own_b_s, own_b_r, k, 1)
                at_time(7.6, own_last, right_b, own_b_r, k, 0)
                at_time(11, own_last, right_b, own_b_r, k, 1)
            for k in (1 - low, low):
                at_time(4.8, own_second, right_a, own_a_s, own_a_r, k, 0)
                at_time(11.2, own_second, right_a, own_a_s, own_a_r, k, 1)
            at_time(4.81, give_left, 0, 0)
            at_time(11.21, give_left, 0, 1)
            at_time(15, own_last, right_a, own_a_r, low, 0)
            at_time(15.1, give_left, 1, 0)
            at_time(17.7, own_last, right_a, own_a_r, 1 - low, 0)
            at_time(21, own_last, right_a, own_a_r, low, 1)
            at_time(21.1, give_left, 1, 1)
            at_time(23.5, own_last, right_a, own_a_r, 1 - low, 1)
            at_time(1.6, x_first, *xb, 0, 0)
            at_time(4.7, x_first, *xb, 0, 1)
            at_time(7.7, x_first, *xb, 1, 0)
            at_time(11.1, x_first, *xb, 1, 1)
            at_time(15.8, x_first, *xa, 0, 0)
            at_time(15.9, x_first, *xa, 0, 1)
            at_time(23.6, x_first, *xa, 1, 0)
            at_time(23.7, x_first, *xa, 1, 1)
            for k in range(2):
                for m in range(2):
                    nth = 2 * m + k + 1
                    at_time(2 + 1.4 * nth + hop, x_arrive, *xb, k, 0, m)
                    at_time(8 + 1.4 * nth + hop, x_arrive, *xb, k, 1, m)
                    at_time(14 + 1.4 * nth + hop, x_last, *xb, k, m)
                    at_time(19.5 + 2.8 * nth + hop, x_arrive, *xa, k, 0, m)
                    at_time(31 + 2.8 * nth + hop, x_arrive, *xa, k, 1, m)
                    at_time(42.5 + 2.8 * nth + hop, x_last, *xa, k, m)
            at_time(46.8, keep_left)
        at_time(25.2, whole_b)
        at_time(43, finish_b)
        at_time(47, right_ready, xa, range(3))
        late = 56.5
        at_time(late, right_ready, xa, (3,))
        for q in range(PARTS):
            done = z_time_a(4, 0, 1, q) + 0.2
            if done < 49:
                at_time(max(done, 47.1), chunks_a, -3, 4, q, False)
                at_time(late, far_a, q)
                at_time(late + 0.01, finish_a, q)
            elif done < late + 1:
                at_time(late + 0.02, chunks_a, -3, 4, q)
                at_time(late + 0.03, finish_a, q)
            else:
                at_time(max(late + 0.04, z_time_a(2, 1, 1, q) + 0.2), chunks_a, -2, 2, q)
                third = z_time_a(3, 1, 1, q) + 0.2
                at_time(third, chunks_a, -3, -3, q)
                at_time(third, chunks_a, 3, 3, q)
                at_time(done, chunks_a, 4, 4, q)
                at_time(done + 0.01, finish_a, q)
        for _, action in sorted(plan, key=lambda entry: entry[0]):
            action()
        all_sent(sent)

    pl.when(c == 0)(functools.partial(run, 0))
    pl.when(c == 1)(functools.partial(run, 1))
    for half in range(2):
        got(o.at[1, :, pl.ds(half * HALF, HALF)], fin_b_r.at[half])
        for q in range(PARTS):
            got(o.at[2 * half, :, piece(q)], fin_a_r.at[half, q])
    all_sent(first)


def local(data):
    bf16, f32 = jnp.bfloat16, jnp.float32
    sem = pltpu.SemaphoreType.DMA

    def sems(*shape):
        return [sem(shape), sem(shape)]

    return pl.pallas_call(
        kernel,
        out_shape=jax.ShapeDtypeStruct(data.shape, data.dtype),
        in_specs=[pl.BlockSpec(memory_space=pltpu.VMEM)],
        out_specs=pl.BlockSpec(memory_space=pltpu.VMEM),
        scratch_shapes=[
            pltpu.VMEM((NZ, 4, 2, ROWS, COLS), bf16),
            pltpu.VMEM((NX, 2, 4, 2, ROWS, COLS), bf16),
            pltpu.VMEM((NZ, 2, 2, ROWS, COLS), bf16),
            pltpu.VMEM((NX, 2, 4, 2, HALF, COLS), bf16),
            pltpu.VMEM((2, ROWS, 2 * COLS), f32),
            pltpu.VMEM((2, ROWS, 2 * COLS), f32),
            pltpu.VMEM((2, HALF, 2 * COLS), f32),
            pltpu.VMEM((2, 2, ROWS, COLS), bf16),
            pltpu.VMEM((2, 2, HALF, COLS), bf16),
            sem((PARTS,)), sem((2, PARTS)),
            *sems(2, 2, 2), *sems(2, 2, 2), *sems(2, 2), sem((2, 2)),
            *sems(2, 4, 2, 1, PARTS), *sems(2, 4, 2, 2, PARTS),
            *sems(NZ, 2, 1, PARTS), *sems(NZ, 2, 2, PARTS),
            *sems(2, 2, 2, 2, 2), *sems(2, 2, 2, 2, 2),
            *sems(4, 2, 2), *sems(4, 2, 2),
            sem, sem,
            *sems(2, PARTS), *sems(2),
        ],
        compiler_params=pltpu.CompilerParams(collective_id=0, has_side_effects=True, vmem_limit_bytes=48 << 20),
        cost_estimate=pl.CostEstimate(flops=6442450944, bytes_accessed=1572864, transcendentals=0),
    )(data)


def solution(mesh):
    spec = P(None, None, "src", "rcv")
    return jax.shard_map(local, mesh=mesh, in_specs=(spec,), out_specs=spec, check_vma=False)
```

```python
import functools

import jax
import jax.numpy as jnp
from jax import lax
from jax.experimental import pallas as pl
from jax.experimental.pallas import tpu as pltpu
from jax.sharding import PartitionSpec as P

MESH = pl.DeviceIdType.MESH
NX, NY, NZ = 4, 4, 8
ROWS, COLS = 512, 128
HALF = ROWS // 2
PARTS = 2
PIECE = ROWS // PARTS


def kernel(d, o, left_a, right_a, left_b, right_b, acc_a, acc_b, part, out_a, out_b,
           own_left_s, own_left_r, own_b_s, own_b_r, own_a_s, own_a_r, give_s, give_r, keep_sem,
           zb_s, zb_r, za_s, za_r, cb_s, cb_r, ca_s, ca_r, xb_s, xb_r, xa_s, xa_r, tb_s, tb_r, ta_s, ta_r,
           part_s, part_r, fin_a_s, fin_a_r, fin_b_s, fin_b_r):
    src, rcv = lax.axis_index("src"), lax.axis_index("rcv")
    x, c = src // 2, src % 2
    z, y = rcv // NY, rcv % NY
    h = y // 2
    low = (y + h) % 2
    pair, across = 2 * h + (y + 1) % 2, NY - 1 - y

    def dev(x, c, z, y):
        return (x * 2 + c, z * NY + y)

    z_next = (dev(x, 0, (z + 1) % NZ, y), dev(x, 0, (z + NZ - 1) % NZ, y))
    x_next = (dev((x + 1) % NX, 1, z, y), dev((x + NX - 1) % NX, 1, z, y))
    partner = dev(x, 1 - c, z, y)

    barrier = pltpu.get_barrier_semaphore()
    friends = [partner]
    for core in range(2):
        friends += [dev((x + 1) % NX, (c + core) % 2, z, y), dev((x + NX - 1) % NX, (c + core) % 2, z, y)]
        friends += [dev(x, (c + core) % 2, (z + 1) % NZ, y), dev(x, (c + core) % 2, (z + NZ - 1) % NZ, y)]
        friends += [dev(x, (c + core) % 2, z, (y + step) % NY) for step in range(1, NY)]
    for friend in friends:
        pl.semaphore_signal(barrier, inc=1, device_id=friend, device_id_type=MESH)
    acc_a[...] = jnp.zeros_like(acc_a)
    acc_b[...] = jnp.zeros_like(acc_b)
    pl.semaphore_wait(barrier, len(friends))

    def piece(q):
        return pl.ds(q * PIECE, PIECE)

    def got(dst_ref, r_sem):
        pltpu.make_async_copy(dst_ref, dst_ref, r_sem).wait()

    def send(sent, src_ref, dst_ref, s_sem, r_sem, device, here=None, local=True):
        copy = pltpu.make_async_remote_copy(
            src_ref=src_ref, dst_ref=dst_ref, send_sem=s_sem, recv_sem=r_sem, device_id=device, device_id_type=MESH)
        if here is None:
            copy.start()
        else:
            pl.when(jnp.logical_not(here))(copy.start)
            if local:
                pl.when(here)(pltpu.make_async_copy(src_ref, dst_ref, r_sem).start)
        sent.append((copy, here))

    def all_sent(sent):
        for copy, here in sent:
            if here is None:
                copy.wait_send()
            else:
                pl.when(jnp.logical_not(here))(copy.wait_send)

    first = []
    stays = low == c
    for direction in range(2):
        send(first, d.at[1, :, pl.ds(h * HALF, HALF)], right_b.at[x, c, y], xb_s.at[direction, 0, c, 0, 0],
             xb_r.at[direction, 0, c, 0, 0], x_next[direction])
    for q in range(PARTS):
        for direction in range(2):
            send(first, d.at[1, :, piece(q)], left_b.at[z, y % 2, :, piece(q)], zb_s.at[direction, 0, 0, 0, q],
                 zb_r.at[direction, 0, 0, 0, q], z_next[direction], low != c, False)
    send(first, d.at[1, :, pl.ds((1 - h) * HALF, HALF)], right_b.at[x, c, y], own_b_s.at[0, 1, 0], own_b_r.at[0, c, 1], dev(x, 1, z, across))
    for q in range(PARTS):
        send(first, d.at[1, :, piece(q)], left_b.at[z, y % 2, :, piece(q)], own_left_s.at[q], own_left_r.at[jnp.where(stays, 0, 1), q],
             dev(x, 0, z, jnp.where(stays, y, pair)), jnp.logical_and(stays, c == 0))
    for q in range(PARTS):
        for direction in range(2):
            send(first, d.at[2 * h, :, piece(q)], left_a.at[z, y, :, piece(q)], za_s.at[direction, 0, 0, 0, q],
                 za_r.at[direction, 0, 0, 0, q], z_next[direction], low != c, False)
    for direction in range(2):
        send(first, d.at[2 * h], right_a.at[x, c, y], xa_s.at[direction, 0, c, 0, 0], xa_r.at[direction, 0, c, 0, 0], x_next[direction])
    send(first, d.at[1, :, pl.ds(h * HALF, HALF)], right_b.at[x, c, y], own_b_s.at[0, 0, 0], own_b_r.at[0, c, 0], dev(x, 1, z, y), c == 1)
    send(first, d.at[2 * (1 - h)], right_a.at[x, c, y], own_a_s.at[0, 1, 0], own_a_r.at[0, c, 1], dev(x, 1, z, across))
    send(first, d.at[2 * h], right_a.at[x, c, y], own_a_s.at[0, 0, 0], own_a_r.at[0, c, 0], dev(x, 1, z, y), c == 1)

    def column(n, m):
        base = y if n == 0 else pair
        return base if m == 0 else NY - 1 - base

    def low_column(n):
        near = jnp.where(h == 0, y, across)
        return near if n == 0 else 1 - near

    def block_b(zz, n, m, q):
        return left_b.at[zz, (y + n) % 2, :, piece(q)]

    def block_a(zz, n, m, q):
        return left_a.at[zz, column(n, m), :, piece(q)]

    zb = (block_b, zb_s, zb_r, cb_s, cb_r)
    za = (block_a, za_s, za_r, ca_s, ca_r)
    xb = (right_b, xb_s, xb_r, tb_s, tb_r)
    xa = (right_a, xa_s, xa_r, ta_s, ta_r)

    def run(core):
        sent = []
        give = functools.partial(send, sent)
        plan = []

        def at_time(time, action, *args):
            plan.append((time, functools.partial(action, *args)))

        def where(block, direction, t, q):
            n, other = t // 2, direction if t % 2 == 0 else 1 - direction
            return (n, 0, other) if block is block_b else (n, other, q)

        def z_first(block, s_sem, r_sem, c_s, c_r, t, q):
            for direction in range(2):
                at = where(block, direction, t, q)
                here = block(z, *at)
                if block is block_b and t % 2 == 0:
                    got(here, own_left_r.at[at[0], at[2]])
                if at[0] or at[1]:
                    give(here, here, s_sem.at[direction, 0, *at], r_sem.at[direction, 0, *at], z_next[direction])
            if block is block_b:
                give(here, here, c_s.at[0, *at], c_r.at[0, *at], partner)

        def z_arrive(block, s_sem, r_sem, c_s, c_r, step, t, q):
            came = []
            for direction in range(2):
                at = where(block, direction, t, q)
                zz = (z + NZ - step) % NZ if direction == 0 else (z + step) % NZ
                here = block(zz, *at)
                got(here, r_sem.at[direction, step - 1, *at])
                if step < 4 - t % 2:
                    give(here, here, s_sem.at[direction, step, *at], r_sem.at[direction, step, *at], z_next[direction])
                came.append((here, NZ - step if direction == 0 else step, at))
            for here, k, at in came:
                give(here, here, c_s.at[k, *at], c_r.at[k, *at], partner)

        def start_b(n):
            for t in (2 * n, 2 * n + 1):
                z_first(*zb, t, 0)

        def take_a(n, m):
            got(left_a.at[z, column(n, m)], give_r.at[n, m])

        def start_a(n, q):
            for t in (2 * n, 2 * n + 1):
                z_first(*za, t, q)

        def left_ready(z_of, k, q):
            block, _, _, _, c_r = z_of
            if core == 1 and (k or block is block_b):
                for n in range(2):
                    for m in range(1 if block is block_b else 2):
                        got(block((z + k) % NZ, n, m, q), c_r.at[k, n, m, q])

        def own_second(right, s_sem, r_sem, k, m):
            here = right.at[x, k, column(0, m)]
            got(here, r_sem.at[0, k, m])
            give(here, here, s_sem.at[1, k, m], r_sem.at[1, k, m], dev(x, c, z, pair))

        def own_last(right, r_sem, k, m):
            got(right.at[x, k, column(1, m)], r_sem.at[1, k, m])

        def pass_on(right, t_s, t_r, slot, xx, k, n):
            here = right.at[xx, k, low_column(n)]
            give(here, here, t_s.at[slot, k, n], t_r.at[slot, k, n], partner)

        def x_first(right, s_sem, r_sem, t_s, t_r, n, m):
            for k in range(2):
                here = right.at[x, k, column(n, m)]
                for direction in range(2 if n or m else 0):
                    give(here, here, s_sem.at[direction, 0, k, n, m], r_sem.at[direction, 0, k, n, m], x_next[direction])
                if m == 1:
                    pass_on(right, t_s, t_r, 0, x, k, n)

        def x_arrive(right, s_sem, r_sem, t_s, t_r, k, n, m):
            for direction in range(2):
                xx = (x + NX - 1) % NX if direction == 0 else (x + 1) % NX
                here = right.at[xx, k, column(n, m)]
                got(here, r_sem.at[direction, 0, k, n, m])
                if n == direction:
                    give(here, here, s_sem.at[direction, 1, k, n, m], r_sem.at[direction, 1, k, n, m], x_next[direction])
                if m == 1:
                    pass_on(right, t_s, t_r, 1 + direction, xx, k, n)

        def x_last(right, s_sem, r_sem, t_s, t_r, k, m):
            xx = (x + 2) % NX
            for n in range(2):
                got(right.at[xx, k, column(n, m)], r_sem.at[n, 1, k, n, m])
                if m == 1:
                    pass_on(right, t_s, t_r, 3, xx, k, n)

        def give_left(n, m):
            here, there = right_a.at[x, low, column(n, m)], left_a.at[z, column(n, m)]
            give(here, there, give_s.at[n, m], give_r.at[n, m], partner)
            pltpu.make_async_copy(here, there, keep_sem.at[n, m]).start()

        def keep_left():
            for n in range(2):
                for m in range(2):
                    got(left_a.at[z, column(n, m)], keep_sem.at[n, m])

        def right_ready(x_of, slots):
            if core == 0:
                right, _, _, _, t_r = x_of
                for slot in slots:
                    for k in range(2):
                        for n in range(2):
                            got(right.at[(x + (0, 3, 1, 2)[slot]) % NX, k, low_column(n)], t_r.at[slot, k, n])

        def multiply(left, width, right, acc, zz, start, rows):
            xx, k = zz // 2, zz % 2
            at = pl.ds(start, rows)
            lr = jnp.concatenate([left[zz, j, 0, at, :] for j in range(width)], axis=1)
            li = jnp.concatenate([left[zz, j, 1, at, :] for j in range(width)], axis=1)
            rr = jnp.concatenate([right[xx, k, 2 * core + p, 0] for p in range(2)], axis=1)
            ri = jnp.concatenate([right[xx, k, 2 * core + p, 1] for p in range(2)], axis=1)

            def dot(a, b):
                return jnp.dot(a, b, preferred_element_type=jnp.float32)

            acc[0, at, :] += dot(lr, rr) - dot(li, ri)
            acc[1, at, :] += dot(lr, ri) + dot(li, rr)

        def whole_b():
            for k in range(NZ):
                for q in range(PARTS):
                    left_ready(zb, k, q)
            right_ready(xb, range(4))

            def one(k, _):
                for q in range(2):
                    multiply(left_b, 2, right_b, acc_b, (z + k) % NZ, q * HALF, HALF)
                return 0

            lax.fori_loop(0, NZ, one, 0)
            give(acc_b.at[:, pl.ds((1 - h) * HALF, HALF)], part, part_s, part_r, dev(x, c, z, across))

        def finish_b():
            got(part, part_r)
            for p in range(2):
                for i in range(2):
                    at = pl.ds(p * COLS, COLS)
                    out_b[p, i] = (acc_b[i, pl.ds(pl.multiple_of(h * HALF, HALF), HALF), at] + part[i, :, at]).astype(jnp.bfloat16)
                give(out_b.at[p], o.at[1, :, pl.ds(h * HALF, HALF)], fin_b_s.at[p], fin_b_r.at[h],
                     dev(x, low, z, 2 * c + p), jnp.logical_and(low == c, y == 2 * c + p))

        def chunks_a(start, stop, q, want=None):
            for k in range(start, stop + 1):
                left_ready(za, k % NZ, q)

            def one(k, _):
                zz = (z + k + start % NZ) % NZ
                if want is None:
                    multiply(left_a, 4, right_a, acc_a, zz, q * PIECE, PIECE)
                else:
                    far = (zz // 2 + NX - x) % NX == 2
                    pl.when(far if want else jnp.logical_not(far))(lambda: multiply(left_a, 4, right_a, acc_a, zz, q * PIECE, PIECE))
                return 0

            lax.fori_loop(0, stop + 1 - start, one, 0)

        def far_a(q):
            def one(k, _):
                multiply(left_a, 4, right_a, acc_a, ((x + 2) % NX) * 2 + k, q * PIECE, PIECE)
                return 0

            lax.fori_loop(0, 2, one, 0)

        def finish_a(q):
            for p in range(2):
                for i in range(2):
                    out_a[p, i, piece(q)] = acc_a[i, piece(q), pl.ds(p * COLS, COLS)].astype(jnp.bfloat16)
                give(out_a.at[p, :, piece(q)], o.at[2 * h, :, piece(q)], fin_a_s.at[p, q], fin_a_r.at[h, q],
                     dev(x, low, z, 2 * c + p), jnp.logical_and(low == c, y == 2 * c + p))

        hop = 1.9
        sub = 39.4 / PARTS
        begin_b = 3.1
        begin_a = 21.4

        ahead = sub / 3.5

        def done_of(step, t):
            return (t + 1 if step < 4 else t // 2 + 1) / 4

        def z_time_b(step, t):
            return (begin_b if step > 1 or t > 1 else 0.3) + 5.6 * (step - 1 + done_of(step, t)) + hop

        def z_time_a(step, t, q):
            if q < PARTS - 1:
                late_by = ahead if q == PARTS - 2 and step > 1 else 0
                return begin_a + sub * q + ahead * (step - 1 + done_of(step, t)) + hop + late_by
            if step == 1:
                return begin_a + sub * q + ahead * (1 + t / 4) - 2.5
            return begin_a + sub * q + ahead * (step - 1 + done_of(step, t)) + hop

        if core == 0:
            at_time(3, start_b, 0)
            at_time(5, start_b, 1)
            for m in range(2):
                at_time(17.4 + m / 100, take_a, 0, m)
                at_time(21.5 + m / 100, take_a, 1, m)
            for q in range(PARTS):
                first_time = 0 if q == 0 else begin_a + sub * (q - 1) + 2.5
                at_time(max(17.5, first_time), start_a, 0, q)
                at_time(max(21.6, first_time + 0.01), start_a, 1, q)
            for step in range(1, 5):
                for t in range(4) if step < 4 else (0, 2):
                    at_time(z_time_b(step, t), z_arrive, *zb, step, t, 0)
                    for q in range(PARTS):
                        at_time(z_time_a(step, t, q), z_arrive, *za, step, t, q)
        else:
            for k in range(2):
                at_time(1.5, own_second, right_b, own_b_s, own_b_r, k, 0)
                at_time(4.6, own_second, right_b, own_b_s, own_b_r, k, 1)
                at_time(7.6, own_last, right_b, own_b_r, k, 0)
                at_time(11, own_last, right_b, own_b_r, k, 1)
            for k in (1 - low, low):
                at_time(4.8, own_second, right_a, own_a_s, own_a_r, k, 0)
                at_time(11.2, own_second, right_a, own_a_s, own_a_r, k, 1)
            at_time(4.81, give_left, 0, 0)
            at_time(11.21, give_left, 0, 1)
            at_time(15, own_last, right_a, own_a_r, low, 0)
            at_time(15.1, give_left, 1, 0)
            at_time(17.7, own_last, right_a, own_a_r, 1 - low, 0)
            at_time(21, own_last, right_a, own_a_r, low, 1)
            at_time(21.1, give_left, 1, 1)
            at_time(23.5, own_last, right_a, own_a_r, 1 - low, 1)
            at_time(1.6, x_first, *xb, 0, 0)
            at_time(4.7, x_first, *xb, 0, 1)
            at_time(7.7, x_first, *xb, 1, 0)
            at_time(11.1, x_first, *xb, 1, 1)
            at_time(17.3, x_first, *xa, 0, 0)
            at_time(17.31, x_first, *xa, 0, 1)
            at_time(23.6, x_first, *xa, 1, 0)
            at_time(23.7, x_first, *xa, 1, 1)
            for k in range(2):
                at_time(5.2, x_arrive, *xb, k, 0, 0)
                at_time(8.7 + 1.4 * (k + 1) + hop, x_arrive, *xb, k, 0, 1)
                at_time(27, x_arrive, *xa, k, 0, 0)
                at_time(22.7 + 2.8 * (k + 1) + hop, x_arrive, *xa, k, 0, 1)
                for m in range(2):
                    nth = 2 * m + k + 1
                    at_time(11.5 + 1.4 * nth + hop, x_arrive, *xb, k, 1, m)
                    at_time(17.1 + 1.4 * nth + hop, x_last, *xb, k, m)
                    at_time(28.3 + 2.8 * nth + hop, x_arrive, *xa, k, 1, m)
                    at_time(39.6 + 2.8 * nth + hop, x_last, *xa, k, m)
            at_time(46.8, keep_left)
        at_time(29, whole_b)
        at_time(50, finish_b)
        at_time(53, right_ready, xa, range(3))
        late = 60
        at_time(late, right_ready, xa, (3,))
        for q in range(PARTS):
            done = z_time_a(4, 2, q) + 0.2
            if done < 49:
                at_time(max(done, 53.1), chunks_a, -3, 4, q, False)
                at_time(late, far_a, q)
                at_time(late + 0.01, finish_a, q)
            elif done < late + 1:
                at_time(late + 0.02, chunks_a, -3, 4, q)
                at_time(late + 0.03, finish_a, q)
            else:
                at_time(max(late + 0.04, z_time_a(2, 3, q) + 0.2), chunks_a, -2, 2, q)
                third = z_time_a(3, 3, q) + 0.2
                at_time(third, chunks_a, -3, -3, q)
                at_time(third, chunks_a, 3, 3, q)
                at_time(done, chunks_a, 4, 4, q)
                at_time(done + 0.01, finish_a, q)
        for _, action in sorted(plan, key=lambda entry: entry[0]):
            action()
        all_sent(sent)

    pl.when(c == 0)(functools.partial(run, 0))
    pl.when(c == 1)(functools.partial(run, 1))
    for half in range(2):
        got(o.at[1, :, pl.ds(half * HALF, HALF)], fin_b_r.at[half])
        for q in range(PARTS):
            got(o.at[2 * half, :, piece(q)], fin_a_r.at[half, q])
    all_sent(first)


def local(data):
    bf16, f32 = jnp.bfloat16, jnp.float32
    sem = pltpu.SemaphoreType.DMA

    def sems(*shape):
        return [sem(shape), sem(shape)]

    return pl.pallas_call(
        kernel,
        out_shape=jax.ShapeDtypeStruct(data.shape, data.dtype),
        in_specs=[pl.BlockSpec(memory_space=pltpu.VMEM)],
        out_specs=pl.BlockSpec(memory_space=pltpu.VMEM),
        scratch_shapes=[
            pltpu.VMEM((NZ, 4, 2, ROWS, COLS), bf16),
            pltpu.VMEM((NX, 2, 4, 2, ROWS, COLS), bf16),
            pltpu.VMEM((NZ, 2, 2, ROWS, COLS), bf16),
            pltpu.VMEM((NX, 2, 4, 2, HALF, COLS), bf16),
            pltpu.VMEM((2, ROWS, 2 * COLS), f32),
            pltpu.VMEM((2, ROWS, 2 * COLS), f32),
            pltpu.VMEM((2, HALF, 2 * COLS), f32),
            pltpu.VMEM((2, 2, ROWS, COLS), bf16),
            pltpu.VMEM((2, 2, HALF, COLS), bf16),
            sem((PARTS,)), sem((2, PARTS)),
            *sems(2, 2, 2), *sems(2, 2, 2), *sems(2, 2), sem((2, 2)),
            *sems(2, 4, 2, 1, PARTS), *sems(2, 4, 2, 2, PARTS),
            *sems(NZ, 2, 1, PARTS), *sems(NZ, 2, 2, PARTS),
            *sems(2, 2, 2, 2, 2), *sems(2, 2, 2, 2, 2),
            *sems(4, 2, 2), *sems(4, 2, 2),
            sem, sem,
            *sems(2, PARTS), *sems(2),
        ],
        compiler_params=pltpu.CompilerParams(collective_id=0, has_side_effects=True, vmem_limit_bytes=48 << 20),
        cost_estimate=pl.CostEstimate(flops=6442450944, bytes_accessed=1572864, transcendentals=0),
    )(data)


def solution(mesh):
    spec = P(None, None, "src", "rcv")
    return jax.shard_map(local, mesh=mesh, in_specs=(spec,), out_specs=spec, check_vma=False)
```

```python
import functools

import jax
import jax.numpy as jnp
from jax import lax
from jax.experimental import pallas as pl
from jax.experimental.pallas import tpu as pltpu
from jax.sharding import PartitionSpec as P

MESH = pl.DeviceIdType.MESH
NX, NY, NZ = 4, 4, 8
ROWS, COLS = 512, 128
HALF = ROWS // 2
PARTS = 2
PIECE = ROWS // PARTS


def kernel(d, o, left_a, right_a, left_b, right_b, acc_a, acc_b, part, out_a, out_b,
           own_left_s, own_left_r, own_b_s, own_b_r, own_a_s, own_a_r, give_s, give_r, keep_sem,
           zb_s, zb_r, za_s, za_r, cb_s, cb_r, ca_s, ca_r, xb_s, xb_r, xa_s, xa_r, tb_s, tb_r, ta_s, ta_r,
           part_s, part_r, fin_a_s, fin_a_r, fin_b_s, fin_b_r):
    src, rcv = lax.axis_index("src"), lax.axis_index("rcv")
    x, c = src // 2, src % 2
    z, y = rcv // NY, rcv % NY
    h = y // 2
    low = (y + h) % 2
    pair, across = 2 * h + (y + 1) % 2, NY - 1 - y

    def dev(x, c, z, y):
        return (x * 2 + c, z * NY + y)

    z_next = (dev(x, 0, (z + 1) % NZ, y), dev(x, 0, (z + NZ - 1) % NZ, y))
    x_next = (dev((x + 1) % NX, 1, z, y), dev((x + NX - 1) % NX, 1, z, y))
    partner = dev(x, 1 - c, z, y)

    barrier = pltpu.get_barrier_semaphore()
    friends = [partner]
    for core in range(2):
        friends += [dev((x + 1) % NX, (c + core) % 2, z, y), dev((x + NX - 1) % NX, (c + core) % 2, z, y)]
        friends += [dev(x, (c + core) % 2, (z + 1) % NZ, y), dev(x, (c + core) % 2, (z + NZ - 1) % NZ, y)]
        friends += [dev(x, (c + core) % 2, z, (y + step) % NY) for step in range(1, NY)]
    for friend in friends:
        pl.semaphore_signal(barrier, inc=1, device_id=friend, device_id_type=MESH)
    acc_a[...] = jnp.zeros_like(acc_a)
    acc_b[...] = jnp.zeros_like(acc_b)
    pl.semaphore_wait(barrier, len(friends))

    def piece(q):
        return pl.ds(q * PIECE, PIECE)

    def got(dst_ref, r_sem):
        pltpu.make_async_copy(dst_ref, dst_ref, r_sem).wait()

    def send(sent, src_ref, dst_ref, s_sem, r_sem, device, here=None, local=True):
        copy = pltpu.make_async_remote_copy(
            src_ref=src_ref, dst_ref=dst_ref, send_sem=s_sem, recv_sem=r_sem, device_id=device, device_id_type=MESH)
        if here is None:
            copy.start()
        else:
            pl.when(jnp.logical_not(here))(copy.start)
            if local:
                pl.when(here)(pltpu.make_async_copy(src_ref, dst_ref, r_sem).start)
        sent.append((copy, here))

    def all_sent(sent):
        for copy, here in sent:
            if here is None:
                copy.wait_send()
            else:
                pl.when(jnp.logical_not(here))(copy.wait_send)

    first = []
    stays = low == c
    for direction in range(2):
        send(first, d.at[1, :, pl.ds(h * HALF, HALF)], right_b.at[x, c, y], xb_s.at[direction, 0, c, 0, 0],
             xb_r.at[direction, 0, c, 0, 0], x_next[direction])
    for q in range(PARTS):
        for direction in range(2):
            send(first, d.at[1, :, piece(q)], left_b.at[z, y % 2, :, piece(q)], zb_s.at[direction, 0, 0, 0, q],
                 zb_r.at[direction, 0, 0, 0, q], z_next[direction], low != c, False)
    send(first, d.at[1, :, pl.ds((1 - h) * HALF, HALF)], right_b.at[x, c, y], own_b_s.at[0, 1, 0], own_b_r.at[0, c, 1], dev(x, 1, z, across))
    for q in range(PARTS):
        send(first, d.at[1, :, piece(q)], left_b.at[z, y % 2, :, piece(q)], own_left_s.at[q], own_left_r.at[jnp.where(stays, 0, 1), q],
             dev(x, 0, z, jnp.where(stays, y, pair)), jnp.logical_and(stays, c == 0))
    for q in range(PARTS):
        for direction in range(2):
            send(first, d.at[2 * h, :, piece(q)], left_a.at[z, y, :, piece(q)], za_s.at[direction, 0, 0, 0, q],
                 za_r.at[direction, 0, 0, 0, q], z_next[direction], low != c, False)
    for direction in range(2):
        send(first, d.at[2 * h], right_a.at[x, c, y], xa_s.at[direction, 0, c, 0, 0], xa_r.at[direction, 0, c, 0, 0], x_next[direction])
    send(first, d.at[1, :, pl.ds(h * HALF, HALF)], right_b.at[x, c, y], own_b_s.at[0, 0, 0], own_b_r.at[0, c, 0], dev(x, 1, z, y), c == 1)
    send(first, d.at[2 * (1 - h)], right_a.at[x, c, y], own_a_s.at[0, 1, 0], own_a_r.at[0, c, 1], dev(x, 1, z, across))
    send(first, d.at[2 * h], right_a.at[x, c, y], own_a_s.at[0, 0, 0], own_a_r.at[0, c, 0], dev(x, 1, z, y), c == 1)

    def column(n, m):
        base = y if n == 0 else pair
        return base if m == 0 else NY - 1 - base

    def low_column(n):
        near = jnp.where(h == 0, y, across)
        return near if n == 0 else 1 - near

    def block_b(zz, n, m, q):
        return left_b.at[zz, (y + n) % 2, :, piece(q)]

    def block_a(zz, n, m, q):
        return left_a.at[zz, column(n, m), :, piece(q)]

    zb = (block_b, zb_s, zb_r, cb_s, cb_r)
    za = (block_a, za_s, za_r, ca_s, ca_r)
    xb = (right_b, xb_s, xb_r, tb_s, tb_r)
    xa = (right_a, xa_s, xa_r, ta_s, ta_r)

    def run(core):
        sent = []
        give = functools.partial(send, sent)
        plan = []

        def at_time(time, action, *args):
            plan.append((time, functools.partial(action, *args)))

        def where(block, direction, t, q):
            n, other = t // 2, direction if t % 2 == 0 else 1 - direction
            return (n, 0, other) if block is block_b else (n, other, q)

        def z_first(block, s_sem, r_sem, c_s, c_r, t, q):
            for direction in range(2):
                at = where(block, direction, t, q)
                here = block(z, *at)
                if block is block_b and t % 2 == 0:
                    got(here, own_left_r.at[at[0], at[2]])
                if at[0] or at[1]:
                    give(here, here, s_sem.at[direction, 0, *at], r_sem.at[direction, 0, *at], z_next[direction])
            if block is block_b:
                give(here, here, c_s.at[0, *at], c_r.at[0, *at], partner)

        def z_arrive(block, s_sem, r_sem, c_s, c_r, step, t, q):
            came = []
            for direction in range(2):
                at = where(block, direction, t, q)
                zz = (z + NZ - step) % NZ if direction == 0 else (z + step) % NZ
                here = block(zz, *at)
                got(here, r_sem.at[direction, step - 1, *at])
                if step < 4 - t % 2:
                    give(here, here, s_sem.at[direction, step, *at], r_sem.at[direction, step, *at], z_next[direction])
                came.append((here, NZ - step if direction == 0 else step, at))
            for here, k, at in came:
                give(here, here, c_s.at[k, *at], c_r.at[k, *at], partner)

        def start_b(n):
            for t in (2 * n, 2 * n + 1):
                z_first(*zb, t, 0)

        def take_a(n, m):
            got(left_a.at[z, column(n, m)], give_r.at[n, m])

        def start_a(n, q):
            for t in (2 * n, 2 * n + 1):
                z_first(*za, t, q)

        def left_ready(z_of, k, q):
            block, _, _, _, c_r = z_of
            if core == 1 and (k or block is block_b):
                for n in range(2):
                    for m in range(1 if block is block_b else 2):
                        got(block((z + k) % NZ, n, m, q), c_r.at[k, n, m, q])

        def own_second(right, s_sem, r_sem, k, m):
            here = right.at[x, k, column(0, m)]
            got(here, r_sem.at[0, k, m])
            give(here, here, s_sem.at[1, k, m], r_sem.at[1, k, m], dev(x, c, z, pair))

        def own_last(right, r_sem, k, m):
            got(right.at[x, k, column(1, m)], r_sem.at[1, k, m])

        def pass_on(right, t_s, t_r, slot, xx, k, n):
            here = right.at[xx, k, low_column(n)]
            give(here, here, t_s.at[slot, k, n], t_r.at[slot, k, n], partner)

        def x_first(right, s_sem, r_sem, t_s, t_r, n, m):
            for k in range(2):
                here = right.at[x, k, column(n, m)]
                for direction in range(2 if n or m else 0):
                    give(here, here, s_sem.at[direction, 0, k, n, m], r_sem.at[direction, 0, k, n, m], x_next[direction])
                if m == 1:
                    pass_on(right, t_s, t_r, 0, x, k, n)

        def x_arrive(right, s_sem, r_sem, t_s, t_r, k, n, m):
            for direction in range(2):
                xx = (x + NX - 1) % NX if direction == 0 else (x + 1) % NX
                here = right.at[xx, k, column(n, m)]
                got(here, r_sem.at[direction, 0, k, n, m])
                if n == direction:
                    give(here, here, s_sem.at[direction, 1, k, n, m], r_sem.at[direction, 1, k, n, m], x_next[direction])
                if m == 1:
                    pass_on(right, t_s, t_r, 1 + direction, xx, k, n)

        def x_last(right, s_sem, r_sem, t_s, t_r, k, m):
            xx = (x + 2) % NX
            for n in range(2):
                got(right.at[xx, k, column(n, m)], r_sem.at[n, 1, k, n, m])
                if m == 1:
                    pass_on(right, t_s, t_r, 3, xx, k, n)

        def give_left(n, m):
            here, there = right_a.at[x, low, column(n, m)], left_a.at[z, column(n, m)]
            give(here, there, give_s.at[n, m], give_r.at[n, m], partner)
            pltpu.make_async_copy(here, there, keep_sem.at[n, m]).start()

        def keep_left():
            for n in range(2):
                for m in range(2):
                    got(left_a.at[z, column(n, m)], keep_sem.at[n, m])

        def right_ready(x_of, slots):
            if core == 0:
                right, _, _, _, t_r = x_of
                for slot in slots:
                    for k in range(2):
                        for n in range(2):
                            got(right.at[(x + (0, 3, 1, 2)[slot]) % NX, k, low_column(n)], t_r.at[slot, k, n])

        def multiply(left, width, right, acc, zz, start, rows):
            xx, k = zz // 2, zz % 2
            at = pl.ds(start, rows)
            lr = jnp.concatenate([left[zz, j, 0, at, :] for j in range(width)], axis=1)
            li = jnp.concatenate([left[zz, j, 1, at, :] for j in range(width)], axis=1)
            rr = jnp.concatenate([right[xx, k, 2 * core + p, 0] for p in range(2)], axis=1)
            ri = jnp.concatenate([right[xx, k, 2 * core + p, 1] for p in range(2)], axis=1)

            def dot(a, b):
                return jnp.dot(a, b, preferred_element_type=jnp.float32)

            acc[0, at, :] += dot(lr, rr) - dot(li, ri)
            acc[1, at, :] += dot(lr, ri) + dot(li, rr)

        def whole_b():
            for k in range(NZ):
                for q in range(PARTS):
                    left_ready(zb, k, q)
            right_ready(xb, range(4))

            def one(k, _):
                for q in range(2):
                    multiply(left_b, 2, right_b, acc_b, (z + k) % NZ, q * HALF, HALF)
                return 0

            lax.fori_loop(0, NZ, one, 0)
            give(acc_b.at[:, pl.ds((1 - h) * HALF, HALF)], part, part_s, part_r, dev(x, c, z, across))

        def finish_b():
            got(part, part_r)
            for p in range(2):
                for i in range(2):
                    at = pl.ds(p * COLS, COLS)
                    out_b[p, i] = (acc_b[i, pl.ds(pl.multiple_of(h * HALF, HALF), HALF), at] + part[i, :, at]).astype(jnp.bfloat16)
                give(out_b.at[p], o.at[1, :, pl.ds(h * HALF, HALF)], fin_b_s.at[p], fin_b_r.at[h],
                     dev(x, low, z, 2 * c + p), jnp.logical_and(low == c, y == 2 * c + p))

        def chunks_a(start, stop, q, want=None):
            for k in range(start, stop + 1):
                left_ready(za, k % NZ, q)

            def one(k, _):
                zz = (z + k + start % NZ) % NZ
                if want is None:
                    multiply(left_a, 4, right_a, acc_a, zz, q * PIECE, PIECE)
                else:
                    far = (zz // 2 + NX - x) % NX == 2
                    pl.when(far if want else jnp.logical_not(far))(lambda: multiply(left_a, 4, right_a, acc_a, zz, q * PIECE, PIECE))
                return 0

            lax.fori_loop(0, stop + 1 - start, one, 0)

        def far_a(q):
            def one(k, _):
                multiply(left_a, 4, right_a, acc_a, ((x + 2) % NX) * 2 + k, q * PIECE, PIECE)
                return 0

            lax.fori_loop(0, 2, one, 0)

        def finish_a(q):
            for p in range(2):
                for i in range(2):
                    out_a[p, i, piece(q)] = acc_a[i, piece(q), pl.ds(p * COLS, COLS)].astype(jnp.bfloat16)
                give(out_a.at[p, :, piece(q)], o.at[2 * h, :, piece(q)], fin_a_s.at[p, q], fin_a_r.at[h, q],
                     dev(x, low, z, 2 * c + p), jnp.logical_and(low == c, y == 2 * c + p))

        hop = 1.9
        sub = 39.4 / PARTS
        begin_b = 3.1
        begin_a = 21.4

        ahead = sub / 3.5

        def done_of(step, t):
            return (t + 1 if step < 4 else t // 2 + 1) / 4

        def z_time_b(step, t):
            return (begin_b if step > 1 or t > 1 else 0.3) + 5.6 * (step - 1 + done_of(step, t)) + hop

        def z_time_a(step, t, q):
            if q < PARTS - 1:
                late_by = ahead if q == PARTS - 2 and step > 1 else 0
                return begin_a + sub * q + ahead * (step - 1 + done_of(step, t)) + hop + late_by
            if step == 1:
                return begin_a + sub * q + ahead * (1 + t / 4) - 2.5
            return begin_a + sub * q + ahead * (step - 1 + done_of(step, t)) + hop

        if core == 0:
            at_time(3, start_b, 0)
            at_time(5, start_b, 1)
            for m in range(2):
                at_time(17.4 + m / 100, take_a, 0, m)
                at_time(21.5 + m / 100, take_a, 1, m)
            for q in range(PARTS):
                first_time = 0 if q == 0 else begin_a + sub * (q - 1) + 2.5
                at_time(max(17.5, first_time), start_a, 0, q)
                at_time(max(21.6, first_time + 0.01), start_a, 1, q)
            for step in range(1, 5):
                for t in range(4) if step < 4 else (0, 2):
                    at_time(z_time_b(step, t), z_arrive, *zb, step, t, 0)
                    for q in range(PARTS):
                        at_time(z_time_a(step, t, q), z_arrive, *za, step, t, q)
        else:
            for k in range(2):
                at_time(1.5, own_second, right_b, own_b_s, own_b_r, k, 0)
                at_time(4.6, own_second, right_b, own_b_s, own_b_r, k, 1)
                at_time(7.6, own_last, right_b, own_b_r, k, 0)
                at_time(11, own_last, right_b, own_b_r, k, 1)
            for k in (1 - low, low):
                at_time(4.8, own_second, right_a, own_a_s, own_a_r, k, 0)
                at_time(11.2, own_second, right_a, own_a_s, own_a_r, k, 1)
            at_time(4.81, give_left, 0, 0)
            at_time(11.21, give_left, 0, 1)
            at_time(15, own_last, right_a, own_a_r, low, 0)
            at_time(15.1, give_left, 1, 0)
            at_time(17.7, own_last, right_a, own_a_r, 1 - low, 0)
            at_time(21, own_last, right_a, own_a_r, low, 1)
            at_time(21.1, give_left, 1, 1)
            at_time(23.5, own_last, right_a, own_a_r, 1 - low, 1)
            at_time(1.6, x_first, *xb, 0, 0)
            at_time(4.7, x_first, *xb, 0, 1)
            at_time(7.7, x_first, *xb, 1, 0)
            at_time(11.1, x_first, *xb, 1, 1)
            at_time(17.3, x_first, *xa, 0, 0)
            at_time(17.31, x_first, *xa, 0, 1)
            at_time(23.6, x_first, *xa, 1, 0)
            at_time(23.7, x_first, *xa, 1, 1)
            for k in range(2):
                at_time(5.2, x_arrive, *xb, k, 0, 0)
                at_time(8.7 + 1.4 * (k + 1) + hop, x_arrive, *xb, k, 0, 1)
                at_time(27, x_arrive, *xa, k, 0, 0)
                at_time(22.7 + 2.8 * (k + 1) + hop, x_arrive, *xa, k, 0, 1)
                for m in range(2):
                    nth = 2 * m + k + 1
                    at_time(11.5 + 1.4 * nth + hop, x_arrive, *xb, k, 1, m)
                    at_time(17.1 + 1.4 * nth + hop, x_last, *xb, k, m)
                    at_time(28.3 + 2.8 * nth + hop, x_arrive, *xa, k, 1, m)
                    at_time(39.6 + 2.8 * nth + hop, x_last, *xa, k, m)
            at_time(46.8, keep_left)
        at_time(29, whole_b)
        at_time(50, finish_b)
        at_time(53, right_ready, xa, range(3))
        late = 60
        at_time(late, right_ready, xa, (3,))
        for q in range(PARTS):
            done = z_time_a(4, 2, q) + 0.2
            if done < 49:
                at_time(max(done, 53.1), chunks_a, -3, 4, q, False)
                at_time(late, far_a, q)
                at_time(late + 0.01, finish_a, q)
            elif done < late + 1:
                at_time(late + 0.02, chunks_a, -3, 4, q)
                at_time(late + 0.03, finish_a, q)
            else:
                at_time(max(late + 0.04, z_time_a(2, 3, q) + 0.2), chunks_a, -2, 2, q)
                third = z_time_a(3, 3, q) + 0.2
                at_time(third, chunks_a, -3, -3, q)
                at_time(third, chunks_a, 3, 3, q)
                at_time(done, chunks_a, 4, 4, q)
                at_time(done + 0.01, finish_a, q)
        for _, action in sorted(plan, key=lambda entry: entry[0]):
            action()
        all_sent(sent)

    pl.when(c == 0)(functools.partial(run, 0))
    pl.when(c == 1)(functools.partial(run, 1))
    for half in range(2):
        got(o.at[1, :, pl.ds(half * HALF, HALF)], fin_b_r.at[half])
        for q in range(PARTS):
            got(o.at[2 * half, :, piece(q)], fin_a_r.at[half, q])
    all_sent(first)


def local(data):
    bf16, f32 = jnp.bfloat16, jnp.float32
    sem = pltpu.SemaphoreType.DMA

    def sems(*shape):
        return [sem(shape), sem(shape)]

    return pl.pallas_call(
        kernel,
        out_shape=jax.ShapeDtypeStruct(data.shape, data.dtype),
        in_specs=[pl.BlockSpec(memory_space=pltpu.HBM)],
        out_specs=pl.BlockSpec(memory_space=pltpu.VMEM),
        scratch_shapes=[
            pltpu.VMEM((NZ, 4, 2, ROWS, COLS), bf16),
            pltpu.VMEM((NX, 2, 4, 2, ROWS, COLS), bf16),
            pltpu.VMEM((NZ, 2, 2, ROWS, COLS), bf16),
            pltpu.VMEM((NX, 2, 4, 2, HALF, COLS), bf16),
            pltpu.VMEM((2, ROWS, 2 * COLS), f32),
            pltpu.VMEM((2, ROWS, 2 * COLS), f32),
            pltpu.VMEM((2, HALF, 2 * COLS), f32),
            pltpu.VMEM((2, 2, ROWS, COLS), bf16),
            pltpu.VMEM((2, 2, HALF, COLS), bf16),
            sem((PARTS,)), sem((2, PARTS)),
            *sems(2, 2, 2), *sems(2, 2, 2), *sems(2, 2), sem((2, 2)),
            *sems(2, 4, 2, 1, PARTS), *sems(2, 4, 2, 2, PARTS),
            *sems(NZ, 2, 1, PARTS), *sems(NZ, 2, 2, PARTS),
            *sems(2, 2, 2, 2, 2), *sems(2, 2, 2, 2, 2),
            *sems(4, 2, 2), *sems(4, 2, 2),
            sem, sem,
            *sems(2, PARTS), *sems(2),
        ],
        compiler_params=pltpu.CompilerParams(collective_id=0, has_side_effects=True, vmem_limit_bytes=48 << 20),
        cost_estimate=pl.CostEstimate(flops=6442450944, bytes_accessed=1572864, transcendentals=0),
    )(data)


def solution(mesh):
    spec = P(None, None, "src", "rcv")
    return jax.shard_map(local, mesh=mesh, in_specs=(spec,), out_specs=spec, check_vma=False)
```
